32 devices in a mesh: groups: 1, gx: 8 (over z, y), gy: 2 (over core), segment: 2 (over x).
Axes of the slice: x: 2, y: 2, z: 4, core: 2. Of those that a mesh axis runs over, the one named last changes fastest.
Arguments:
- activations: bfloat16 [2, 8, 128, 128, 128], P('segment', 'groups', 'gx', 'gy'), may hold values from -6 to 6
- cotangent: bfloat16 [8, 128, 128, 128], P('groups', 'gx', 'gy'), may hold values from -6 to 6
- spectral_weights: float32 [2, 32, 32, 8, 8, 32], P('segment', 'gy', 'gx'), may hold values from -6 to 6
- pointwise: float32 [2, 8, 8], P('segment'), may hold values from -2 to 2
- channel_bias: float32 [2, 8], P('segment'), may hold values from -3 to 3
Outputs:
- input_grads: bfloat16 [2, 8, 128, 128, 128], P('segment', 'groups', 'gx', 'gy')
- spectral_grads: float32 [2, 32, 32, 8, 8, 32], P('segment', 'gy', 'gx', 'groups')
The draws below stay inside these ranges and needn't reach their ends.
All inputs are finite; a program needn't handle non-finite values.
Results may differ from the reference program's by a relative error of at most 0.0042.
Values may be sent and summed in bfloat16 or wider, within the bound.
A program may use at most 64 MiB of HBM per device.

```python
import math
import jax
import jax.numpy as jnp
from jax import lax

C = 8
NX = 128
NY = 128
NZ = 128
MODES = 32
SEGMENTS = 2


def levels(key, extent, split, low, high):
    loudness, own = 1.0, jax.random.fold_in(key, 6)
    for axis_at, shards_of in split:
        heights = jnp.exp(jax.random.uniform(jax.random.fold_in(own, axis_at), (shards_of,), jnp.float32, low / len(split), high / len(split)))
        loudness = loudness * jnp.repeat(heights, extent[axis_at] // shards_of).reshape([-1 if axis == axis_at else 1 for axis in range(len(extent))])
    return loudness


def scatter_about(own_key, extent, spread, most, pieces=(), kind=jnp.bfloat16):
    level = levels(own_key, extent, pieces, -0.22, 0.18) if pieces else 1.0
    result = jax.random.normal(own_key, extent, jnp.float32) * spread * level
    return jnp.minimum(jnp.maximum(result, -most), most).astype(kind)


def setup_inputs(seed: int = 0, part: int = 0) -> dict:
    arg_keys = jax.random.split(jax.random.key(seed), 6)
    own_keys = jax.random.split(jax.random.fold_in(arg_keys[5], part), 6)
    activations = scatter_about(own_keys[0], (SEGMENTS, C, NX, NY, NZ), 1.0, 6.0, ((0, 2), (2, 8), (3, 2)))
    cotangent = scatter_about(own_keys[1], (C, NX, NY, NZ), 1.0, 6.0, ((1, 8), (2, 2)))
    spectral_weights = scatter_about(arg_keys[2], (SEGMENTS, MODES, MODES, C, C, MODES), 1.0, 6.0, ((0, 2), (1, 2), (2, 8)), jnp.float32)
    pointwise = scatter_about(arg_keys[3], (SEGMENTS, C, C), C ** -0.5, 2.0, ((0, 2),), jnp.float32)
    channel_bias = scatter_about(arg_keys[4], (SEGMENTS, C), 0.7, 3.0, ((0, 2),), jnp.float32)
    return dict(activations=activations, cotangent=cotangent, spectral_weights=spectral_weights, pointwise=pointwise, channel_bias=channel_bias)


highest = lax.Precision.HIGHEST

def trig_basis(length, mode_count):
    half = mode_count // 2
    freqs = jnp.arange(half, dtype=jnp.int32)[:, None]
    points = jnp.arange(length, dtype=jnp.int32)[None, :]
    step_angle = 2.0 * math.pi / length
    cosine = jnp.cos((freqs * points % length).astype(jnp.float32) * step_angle)
    sine = jnp.sin(((freqs + 1) * points % length).astype(jnp.float32) * step_angle)
    rows_all = jnp.concatenate([cosine, sine], axis=0)
    scales = jnp.where(jnp.arange(mode_count) == 0, 1.0 / math.sqrt(length), math.sqrt(2.0 / length)).astype(jnp.float32)
    return rows_all * scales[:, None]

def to_modes(field, along_x, along_y, along_z):
    inner = jnp.einsum('ixyz,cz->cixy', field, along_z, precision=highest)
    inner = jnp.einsum('cixy,ax->ciay', inner, along_x, precision=highest)
    return jnp.einsum('ciay,jy->jcia', inner, along_y, precision=highest)

def to_field(spectrum, along_x, along_y, along_z):
    inner = jnp.einsum('jcia,jy->ciay', spectrum, along_y, precision=highest)
    inner = jnp.einsum('ciay,ax->cixy', inner, along_x, precision=highest)
    return jnp.einsum('cixy,cz->ixyz', inner, along_z, precision=highest)

def gelu_slope(value):
    normal_cdf = 0.5 * (1.0 + jax.scipy.special.erf(value * 0.7071067811865476))
    return normal_cdf + value * jnp.exp(-0.5 * value * value) * 0.3989422804014327

def reference(activations, cotangent, spectral_weights, pointwise, channel_bias):
    along_x = trig_basis(NX, MODES)
    along_y = trig_basis(NY, MODES)
    along_z = trig_basis(NZ, MODES)
    incoming = cotangent
    grad_fields = []
    weight_grads = []
    for segment_index in range(SEGMENTS - 1, -1, -1):
        inputs = activations[segment_index].astype(jnp.float32)
        weights = spectral_weights[segment_index]
        mixing = pointwise[segment_index]
        input_modes = to_modes(inputs, along_x, along_y, along_z)
        mixed = jnp.einsum('jcioa,jcia->jcoa', weights, input_modes, precision=highest)
        pre_act = jnp.einsum('oi,ixyz->oxyz', mixing, inputs, precision=highest)
        pre_act = pre_act + channel_bias[segment_index][:, None, None, None] + to_field(mixed, along_x, along_y, along_z)
        signal = incoming.astype(jnp.float32) * gelu_slope(pre_act)
        grad_modes = to_modes(signal, along_x, along_y, along_z)
        back = jnp.einsum('jcioa,jcoa->jcia', weights, grad_modes, precision=highest)
        input_grad = jnp.einsum('oi,oxyz->ixyz', mixing, signal, precision=highest) + to_field(back, along_x, along_y, along_z)
        input_grad = input_grad.astype(jnp.bfloat16)
        grad_fields.append(input_grad)
        weight_grads.append(jnp.einsum('jcia,jcoa->jcioa', input_modes, grad_modes, precision=highest))
        incoming = input_grad
    ordered_fields = grad_fields[::-1]
    ordered_weights = weight_grads[::-1]
    return (jnp.stack(ordered_fields), jnp.stack(ordered_weights))
```

```python
import math

import jax
import jax.numpy as jnp
from jax import lax
from jax.sharding import PartitionSpec as P

MODES = 32


highest = lax.Precision.HIGHEST


def from_behind(block, axis, distance):
    devices = range(lax.axis_size(axis))
    route = [(i - distance, i) for i in devices if i - distance in devices]
    return lax.ppermute(block, axis, route)


def trig_basis(length, mode_count):
    half = mode_count // 2
    freqs = jnp.arange(half, dtype=jnp.int32)[:, None]
    points = jnp.arange(length, dtype=jnp.int32)[None, :]
    step_angle = 2.0 * math.pi / length
    cosine = jnp.cos((freqs * points % length).astype(jnp.float32) * step_angle)
    sine = jnp.sin(((freqs + 1) * points % length).astype(jnp.float32) * step_angle)
    rows_all = jnp.concatenate([cosine, sine], axis=0)
    scales = jnp.where(
        jnp.arange(mode_count) == 0, 1.0 / math.sqrt(length), math.sqrt(2.0 / length)
    ).astype(jnp.float32)
    return rows_all * scales[:, None]


def gelu_slope(value):
    normal_cdf = 0.5 * (1.0 + jax.scipy.special.erf(value * 0.7071067811865476))
    return normal_cdf + value * jnp.exp(-0.5 * value * value) * 0.3989422804014327


def channel_mix(matrix, field):
    return jnp.sum(matrix[:, :, None, None, None] * field[None], axis=1)


def body(activations, cotangent, spectral_weights, pointwise, channel_bias):
    inputs = activations[0].astype(jnp.float32)
    channels, rows_x, rows_y, length_z = inputs.shape
    count_x = lax.axis_size("gx")
    count_y = lax.axis_size("gy")
    mode_count = MODES
    along_x = trig_basis(rows_x * count_x, mode_count)
    along_z = trig_basis(length_z, mode_count)
    along_y = lax.dynamic_slice_in_dim(
        trig_basis(rows_y * count_y, mode_count), lax.axis_index("gy") * rows_y, rows_y, 1
    )
    weights = spectral_weights[0]
    mixing = pointwise[0]
    mixing_back = jnp.transpose(mixing)

    own_modes = mode_count // count_y
    own_thirds = mode_count // count_x
    peers = ("gx", "gy")
    high = lax.Precision.HIGH
    along_x_slabs = along_x.reshape(mode_count, count_x, rows_x)

    def analyse(field):
        third = jnp.einsum("ixyz,cz->cixy", field, along_z, precision=high)
        second = jnp.einsum("cixy,jy->jcix", third, along_y, precision=high)
        parts = second.astype(jnp.bfloat16).reshape(
            count_y, own_modes, count_x, own_thirds, channels, rows_x
        )
        parts = jnp.transpose(parts, (2, 0, 1, 3, 4, 5)).reshape(
            count_x * count_y, own_modes * own_thirds * channels * rows_x
        )
        parts = lax.all_to_all(parts, peers, split_axis=0, concat_axis=0, tiled=True)
        parts = parts.reshape(
            count_x, count_y, own_modes, own_thirds, channels, rows_x
        ).astype(jnp.float32)
        return jnp.einsum(
            "sgjcix,asx->jcia", parts, along_x_slabs, precision=high
        )

    def synthesise(spectrum):
        spread = jnp.einsum("jcia,asx->sjcix", spectrum, along_x_slabs, precision=high)
        spread = spread.astype(jnp.bfloat16).reshape(count_x, 1, -1)
        spread = jnp.broadcast_to(
            spread, (count_x, count_y, spread.shape[-1])
        ).reshape(count_x * count_y, -1)
        parts = lax.all_to_all(spread, peers, split_axis=0, concat_axis=0, tiled=True)
        parts = parts.reshape(
            count_x, count_y, own_modes, own_thirds, channels, rows_x
        ).astype(jnp.float32)
        second = jnp.einsum(
            "sgjcix,gjy->scixy",
            parts,
            along_y.reshape(count_y, own_modes, rows_y),
            precision=high,
        )
        return jnp.einsum(
            "cixy,cz->ixyz",
            second.reshape(mode_count, channels, rows_x, rows_y),
            along_z,
            precision=high,
        )

    input_modes = analyse(inputs)
    mixed = jnp.einsum("jcioa,jcia->jcoa", weights, input_modes, precision=highest)
    pre_act = channel_mix(mixing, inputs)
    pre_act = pre_act + channel_bias[0][:, None, None, None] + synthesise(mixed)
    slope_field = gelu_slope(pre_act)
    segment_index = lax.axis_index("segment")
    segment_count = lax.axis_size("segment")
    incoming = cotangent
    kept_grad = jnp.zeros(cotangent.shape, jnp.bfloat16)
    kept_modes = jnp.zeros(input_modes.shape, jnp.float32)
    for turn_index in range(segment_count):
        active = segment_index == segment_count - 1 - turn_index
        signal = incoming.astype(jnp.float32) * slope_field
        grad_modes = analyse(signal)
        back = jnp.einsum("jcioa,jcoa->jcia", weights, grad_modes, precision=highest)
        input_grad = channel_mix(mixing_back, signal) + synthesise(back)
        input_grad = input_grad.astype(jnp.bfloat16)
        kept_grad = jnp.where(active, input_grad, kept_grad)
        kept_modes = jnp.where(active, grad_modes, kept_modes)
        if turn_index + 1 < segment_count:
            incoming = from_behind(input_grad, "segment", -1)
    weight_grad = jnp.einsum("jcia,jcoa->jcioa", input_modes, kept_modes, precision=highest)
    return (kept_grad[None], weight_grad[None])


def solution(mesh):
    return jax.shard_map(
        body,
        mesh=mesh,
        in_specs=(
            P("segment", "groups", "gx", "gy", None),
            P("groups", "gx", "gy", None),
            P("segment", "gy", "gx", None, None, None),
            P("segment", None, None),
            P("segment", None),
        ),
        out_specs=(
            P("segment", "groups", "gx", "gy", None),
            P("segment", "gy", "gx", "groups", None, None),
        ),
        check_vma=False,
    )
```

```python
import functools
import math

import jax
import jax.numpy as jnp
import ml_dtypes
import numpy as np
from jax import lax
from jax.experimental import pallas as pl
from jax.experimental.pallas import tpu as pltpu
from jax.sharding import PartitionSpec as P

MODES = 32
f32, bf16 = jnp.float32, jnp.bfloat16


def from_behind(block, axis, distance):
    devices = range(lax.axis_size(axis))
    route = [(i - distance, i) for i in devices if i - distance in devices]
    return lax.ppermute(block, axis, route)


def trig_basis(length):
    half = MODES // 2
    freqs = np.arange(half)[:, None]
    points = np.arange(length)[None, :]
    step = 2.0 * math.pi / length
    rows = np.concatenate(
        [np.cos((freqs * points % length) * step), np.sin(((freqs + 1) * points % length) * step)]
    )
    scales = np.where(np.arange(MODES) == 0, 1.0 / math.sqrt(length), math.sqrt(2.0 / length))
    return rows * scales[:, None]


def halves(matrix):
    matrix = np.asarray(matrix, np.float32)
    top = matrix.astype(ml_dtypes.bfloat16)
    rest = (matrix - top.astype(np.float32)).astype(ml_dtypes.bfloat16)
    return np.stack([top, rest])


def split(value):
    top = value.astype(bf16)
    return top, (value - top.astype(f32)).astype(bf16)


def dot(a, b, ca=1, cb=0):
    return lax.dot_general(a, b, (((ca,), (cb,)), ((), ())), preferred_element_type=f32)


def kernel(
    back, nx, ny, xr, *refs
):
    if back:
        (inc_ref, slope_ref, w_hbm, mix_ref, bz_ref, bzs_ref, ky_ref, kyt_ref, bx_ref, bxr_ref,
         out_ref, modes_ref, *scratch) = refs
    else:
        (inc_ref, w_hbm, mix_ref, bias_ref, bz_ref, bzs_ref, ky_ref, kyt_ref, bx_ref, bxr_ref,
         out_ref, modes_ref, *scratch) = refs
    (w_ref, sig_ref, ghi_ref, glo_ref, s_ref, r_ref, m_ref, p_ref, q_ref, qs_ref,
     send1, recv1, send2, recv2, wsem) = scratch
    channels, _, yr, zr = inc_ref.shape
    cl, jl, xp = MODES // nx, MODES // ny, r_ref.shape[2]
    n = nx * ny
    lanes = jl * channels
    gx, gy = lax.axis_index("gx"), lax.axis_index("gy")
    me = gx * ny + gy

    wcopy = pltpu.make_async_copy(w_hbm, w_ref, wsem)
    wcopy.start()

    barrier = pltpu.get_barrier_semaphore()

    def greet(k, carry):
        peer = lax.rem(me + k, n)
        pl.semaphore_signal(
            barrier, inc=1,
            device_id={"gx": peer // ny, "gy": lax.rem(peer, ny)},
            device_id_type=pl.DeviceIdType.MESH,
        )
        return carry

    lax.fori_loop(1, n, greet, 0)

    def along_z(x, carry):
        if back:
            signal = inc_ref[:, x].astype(f32) * slope_ref[:, x]
            sig_ref[:, x] = signal
            block = signal.astype(bf16)
        else:
            block = inc_ref[:, x]
        block = block.reshape(channels * yr, zr)
        g = dot(bz_ref[0], block, 1, 1) + dot(bz_ref[1], block, 1, 1)
        ghi, glo = split(g)
        rows = pl.ds(pl.multiple_of(x * MODES, MODES), MODES)
        ghi_ref[rows, :] = ghi
        glo_ref[rows, :] = glo
        return carry

    lax.fori_loop(0, xr, along_z, 0)
    ghi = ghi_ref[...]
    t = dot(ghi, ky_ref[0]) + dot(ghi, ky_ref[1]) + dot(glo_ref[...], ky_ref[0])
    t = jnp.swapaxes(t.reshape(xr, MODES, ny * lanes), 0, 1)
    if xp > xr:
        t = jnp.concatenate([t, jnp.zeros((MODES, xp - xr, ny * lanes), f32)], axis=1)
    t = t.astype(bf16)
    for h in range(ny):
        s_ref[h] = t[:, :, h * lanes : (h + 1) * lanes].reshape(nx, cl, xp, lanes)

    pl.semaphore_wait(barrier, n - 1)

    def exchange(source, target, send, recv):
        def copy_to(peer, slot_of):
            return pltpu.make_async_remote_copy(
                src_ref=source(peer // ny, lax.rem(peer, ny)),
                dst_ref=target.at[lax.rem(slot_of, ny) * nx + slot_of // ny],
                send_sem=send.at[peer],
                recv_sem=recv.at[slot_of],
                device_id={"gx": peer // ny, "gy": lax.rem(peer, ny)},
                device_id_type=pl.DeviceIdType.MESH,
            )

        def begin(k, carry):
            copy_to(lax.rem(me + k, n), me).start()
            return carry

        def finish(k, carry):
            copy_to(lax.rem(me + k, n), me).wait_send()
            peer = lax.rem(me + n - k, n)
            copy_to(peer, peer).wait_recv()
            return carry

        lax.fori_loop(1, n, begin, 0)
        target[gy * nx + gx] = source(gx, gy)[...]
        lax.fori_loop(1, n, finish, 0)

    exchange(lambda d, h: s_ref.at[h, d], r_ref, send1, recv1)

    for c in range(cl):
        part = r_ref[:, c].reshape(n * xp, lanes)
        own = dot(bx_ref[0], part) + dot(bx_ref[1], part)
        modes_ref[c] = own.T.reshape(jl, channels, MODES)
    wcopy.wait()

    def mix(j, carry):
        for c in range(cl):
            own = modes_ref[c, j]
            weight = w_ref[j, c]
            if back:
                m_ref[c, j] = jnp.sum(weight * own[None], axis=1)
            else:
                m_ref[c, j] = jnp.sum(weight * own[:, None, :], axis=0)
        return carry

    lax.fori_loop(0, jl, mix, 0)
    for c in range(cl):
        top, rest = split(m_ref[c].reshape(lanes, MODES))
        spread = (
            dot(bxr_ref[0], top, 1, 1) + dot(bxr_ref[1], top, 1, 1) + dot(bxr_ref[0], rest, 1, 1)
        )
        p_ref[:, c] = spread.astype(bf16).reshape(nx, xp, lanes)

    exchange(lambda d, h: p_ref.at[d], q_ref, send2, recv2)

    got = [q_ref[h * nx : (h + 1) * nx].reshape(MODES, xp, lanes) for h in range(ny)]
    got = jnp.concatenate(got, axis=2).astype(f32)
    got = jnp.swapaxes(got, 0, 1)[:xr].reshape(xr * MODES, ny * lanes).astype(bf16)
    qs_ref[...] = dot(got, kyt_ref[0]) + dot(got, kyt_ref[1])

    def finish_field(x, carry):
        rows = pl.ds(pl.multiple_of(x * MODES, MODES), MODES)
        top, rest = split(qs_ref[rows, :])
        stack = jnp.concatenate([top, rest, top], axis=0)
        field = dot(stack, bzs_ref[...], 0, 0).reshape(channels, yr, zr)
        if back:
            values = [sig_ref[i, x] for i in range(channels)]
        else:
            values = [inc_ref[i, x].astype(f32) for i in range(channels)]
        for o in range(channels):
            total = field[o]
            for i in range(channels):
                total = total + (mix_ref[i, o] if back else mix_ref[o, i]) * values[i]
            if back:
                out_ref[o, x] = total.astype(bf16)
            else:
                total = total + bias_ref[0, o]
                cdf = 0.5 * (1.0 + lax.erf(total * 0.7071067811865476))
                out_ref[o, x] = cdf + total * jnp.exp(-0.5 * total * total) * 0.3989422804014327
        return carry

    lax.fori_loop(0, xr, finish_field, 0)


def block_turn(back, nx, ny, collective, field, slope, weights, mixing, bias, tables):
    channels, xr, yr, zr = field.shape
    xp = -(-xr // 16) * 16
    cl, jl, n = MODES // nx, MODES // ny, nx * ny
    lanes = jl * channels
    vmem = pl.BlockSpec(memory_space=pltpu.VMEM)
    smem = pl.BlockSpec(memory_space=pltpu.SMEM)
    hbm = pl.BlockSpec(memory_space=pl.ANY)
    if back:
        args = (field, slope, weights, mixing, *tables)
        specs = [vmem, vmem, hbm, smem] + [vmem] * len(tables)
    else:
        args = (field, weights, mixing, bias, *tables)
        specs = [vmem, hbm, smem, smem] + [vmem] * len(tables)
    dma = pltpu.SemaphoreType.DMA
    return pl.pallas_call(
        functools.partial(kernel, back, nx, ny, xr),
        out_shape=(
            jax.ShapeDtypeStruct(field.shape, bf16 if back else f32),
            jax.ShapeDtypeStruct((cl, jl, channels, MODES), f32),
        ),
        in_specs=specs,
        out_specs=(vmem, vmem),
        scratch_shapes=[
            pltpu.VMEM(weights.shape, f32),
            pltpu.VMEM(field.shape if back else (8, 128), f32),
            pltpu.VMEM((xr * MODES, channels * yr), bf16),
            pltpu.VMEM((xr * MODES, channels * yr), bf16),
            pltpu.VMEM((ny, nx, cl, xp, lanes), bf16),
            pltpu.VMEM((n, cl, xp, lanes), bf16),
            pltpu.VMEM((cl, jl, channels, MODES), f32),
            pltpu.VMEM((nx, cl, xp, lanes), bf16),
            pltpu.VMEM((n, cl, xp, lanes), bf16),
            pltpu.VMEM((xr * MODES, channels * yr), f32),
            dma((n,)), dma((n,)), dma((n,)), dma((n,)), dma,
        ],
        compiler_params=pltpu.CompilerParams(
            collective_id=collective, has_side_effects=True, vmem_limit_bytes=50 * 2**20
        ),
        cost_estimate=pl.CostEstimate(flops=10**9, bytes_accessed=2 * 10**7, transcendentals=10**6),
    )(*args)


def body(activations, cotangent, spectral_weights, pointwise, channel_bias):
    inputs = activations[0]
    channels, xr, yr, zr = inputs.shape
    nx, ny = lax.axis_size("gx"), lax.axis_size("gy")
    xp = -(-xr // 16) * 16
    bz = trig_basis(zr)
    bx = trig_basis(xr * nx).reshape(MODES, nx, xr)
    bx = np.concatenate([bx, np.zeros((MODES, nx, xp - xr))], axis=2).reshape(MODES, nx * xp)
    by = trig_basis(yr * ny).reshape(MODES, ny, yr)
    kron = np.einsum("jgy,ik->giyjk", by, np.eye(channels)).reshape(
        ny, channels * yr, MODES * channels
    )
    bzh = halves(bz)
    kh = halves(kron)
    gy = lax.axis_index("gy")
    ky = lax.dynamic_index_in_dim(jnp.asarray(np.swapaxes(kh, 0, 1)), gy, 0, False)
    kyt = lax.dynamic_index_in_dim(
        jnp.asarray(np.ascontiguousarray(np.transpose(kh, (1, 0, 3, 2)))), gy, 0, False
    )
    tables = (
        jnp.asarray(bzh),
        jnp.asarray(np.concatenate([bzh[0], bzh[0], bzh[1]], axis=0)),
        ky,
        kyt,
        jnp.asarray(halves(np.concatenate([bx] * ny, axis=1))),
        jnp.asarray(halves(bx.T)),
    )
    weights = spectral_weights[0]
    mixing = pointwise[0]
    slope, input_modes = block_turn(
        False, nx, ny, 0, inputs, None, weights, mixing, channel_bias, tables
    )
    segment_index = lax.axis_index("segment")
    segment_count = lax.axis_size("segment")
    incoming = cotangent
    kept_grad = jnp.zeros(cotangent.shape, bf16)
    kept_modes = jnp.zeros(input_modes.shape, f32)
    for turn_index in range(segment_count):
        active = segment_index == segment_count - 1 - turn_index
        input_grad, grad_modes = block_turn(
            True, nx, ny, 1 + turn_index, incoming, slope, weights, mixing, None, tables
        )
        kept_grad = jnp.where(active, input_grad, kept_grad)
        kept_modes = jnp.where(active, grad_modes, kept_modes)
        if turn_index + 1 < segment_count:
            incoming = from_behind(input_grad, "segment", -1)
    input_modes = jnp.swapaxes(input_modes, 0, 1)
    kept_modes = jnp.swapaxes(kept_modes, 0, 1)
    weight_grad = input_modes[:, :, :, None, :] * kept_modes[:, :, None, :, :]
    return (kept_grad[None], weight_grad[None])


def solution(mesh):
    return jax.shard_map(
        body,
        mesh=mesh,
        in_specs=(
            P("segment", "groups", "gx", "gy", None),
            P("groups", "gx", "gy", None),
            P("segment", "gy", "gx", None, None, None),
            P("segment", None, None),
            P("segment", None),
        ),
        out_specs=(
            P("segment", "groups", "gx", "gy", None),
            P("segment", "gy", "gx", "groups", None, None),
        ),
        check_vma=False,
    )
```

```python
import functools
import math

import jax
import jax.numpy as jnp
import ml_dtypes
import numpy as np
from jax import lax
from jax.experimental import pallas as pl
from jax.experimental.pallas import tpu as pltpu
from jax.sharding import PartitionSpec as P

MODES = 32
f32, bf16 = jnp.float32, jnp.bfloat16


def from_behind(block, axis, distance):
    devices = range(lax.axis_size(axis))
    route = [(i - distance, i) for i in devices if i - distance in devices]
    return lax.ppermute(block, axis, route)


def trig_basis(length):
    half = MODES // 2
    freqs = np.arange(half)[:, None]
    points = np.arange(length)[None, :]
    step = 2.0 * math.pi / length
    rows = np.concatenate(
        [np.cos((freqs * points % length) * step), np.sin(((freqs + 1) * points % length) * step)]
    )
    scales = np.where(np.arange(MODES) == 0, 1.0 / math.sqrt(length), math.sqrt(2.0 / length))
    return rows * scales[:, None]


def halves(matrix):
    matrix = np.asarray(matrix, np.float32)
    top = matrix.astype(ml_dtypes.bfloat16)
    rest = (matrix - top.astype(np.float32)).astype(ml_dtypes.bfloat16)
    return np.stack([top, rest])


def split(value):
    top = value.astype(bf16)
    return top, (value - top.astype(f32)).astype(bf16)


def dot(a, b, ca=1, cb=0):
    return lax.dot_general(a, b, (((ca,), (cb,)), ((), ())), preferred_element_type=f32)


def kernel(
    back, nx, ny, xr, *refs
):
    if back:
        (inc_ref, slope_ref, w_hbm, mix_ref, bz_ref, bzs_ref, ky_ref, kyt_ref, bx_ref, bxr_ref,
         out_ref, modes_ref, got_ref, *scratch) = refs
    else:
        (inc_ref, w_hbm, mix_ref, bias_ref, bz_ref, bzs_ref, ky_ref, kyt_ref, bx_ref, bxr_ref,
         out_ref, modes_ref, got_ref, *scratch) = refs
    (w_ref, sig_ref, ghi_ref, glo_ref, s_ref, r_ref, m_ref, p_ref, q_ref, qs_ref,
     send1, recv1, send2, recv2, wsem) = scratch
    channels, _, yr, zr = inc_ref.shape
    cl, jl, xp = MODES // nx, MODES // ny, r_ref.shape[2]
    n = nx * ny
    lanes = jl * channels
    gx, gy = lax.axis_index("gx"), lax.axis_index("gy")
    me = gx * ny + gy

    wcopy = pltpu.make_async_copy(w_hbm, w_ref, wsem)
    wcopy.start()

    barrier = pltpu.get_barrier_semaphore()

    def greet(k, carry):
        peer = lax.rem(me + k, n)
        pl.semaphore_signal(
            barrier, inc=1,
            device_id={"gx": peer // ny, "gy": lax.rem(peer, ny)},
            device_id_type=pl.DeviceIdType.MESH,
        )
        return carry

    lax.fori_loop(1, n, greet, 0)

    def along_z(x, carry):
        if back:
            signal = inc_ref[:, x].astype(f32) * slope_ref[:, x]
            sig_ref[:, x] = signal
            block = signal.astype(bf16)
        else:
            block = inc_ref[:, x]
        block = block.reshape(channels * yr, zr)
        g = dot(bz_ref[0], block, 1, 1) + dot(bz_ref[1], block, 1, 1)
        ghi, glo = split(g)
        rows = pl.ds(pl.multiple_of(x * MODES, MODES), MODES)
        ghi_ref[rows, :] = ghi
        glo_ref[rows, :] = glo
        return carry

    lax.fori_loop(0, xr, along_z, 0)
    ghi = ghi_ref[...]
    t = dot(ghi, ky_ref[0]) + dot(ghi, ky_ref[1]) + dot(glo_ref[...], ky_ref[0])
    t = jnp.swapaxes(t.reshape(xr, MODES, ny * lanes), 0, 1)
    if xp > xr:
        t = jnp.concatenate([t, jnp.zeros((MODES, xp - xr, ny * lanes), f32)], axis=1)
    t = t.astype(bf16)
    for h in range(ny):
        s_ref[h] = t[:, :, h * lanes : (h + 1) * lanes].reshape(nx, cl, xp, lanes)

    pl.semaphore_wait(barrier, n - 1)

    def exchange(source, target, send, recv):
        def copy_to(peer, slot_of):
            return pltpu.make_async_remote_copy(
                src_ref=source(peer // ny, lax.rem(peer, ny)),
                dst_ref=target.at[lax.rem(slot_of, ny) * nx + slot_of // ny],
                send_sem=send.at[peer],
                recv_sem=recv.at[slot_of],
                device_id={"gx": peer // ny, "gy": lax.rem(peer, ny)},
                device_id_type=pl.DeviceIdType.MESH,
            )

        def begin(k, carry):
            copy_to(lax.rem(me + k, n), me).start()
            return carry

        def finish(k, carry):
            copy_to(lax.rem(me + k, n), me).wait_send()
            peer = lax.rem(me + n - k, n)
            copy_to(peer, peer).wait_recv()
            return carry

        lax.fori_loop(1, n, begin, 0)
        target[gy * nx + gx] = source(gx, gy)[...]
        lax.fori_loop(1, n, finish, 0)

    exchange(lambda d, h: s_ref.at[h, d], r_ref, send1, recv1)

    for c in range(cl):
        part = r_ref[:, c].reshape(n * xp, lanes)
        own = dot(bx_ref[0], part) + dot(bx_ref[1], part)
        modes_ref[c] = own.T.reshape(jl, channels, MODES)
    wcopy.wait()

    def mix(j, carry):
        for c in range(cl):
            own = modes_ref[c, j]
            weight = w_ref[j, c]
            if back:
                m_ref[c, j] = jnp.sum(weight * own[None], axis=1)
            else:
                m_ref[c, j] = jnp.sum(weight * own[:, None, :], axis=0)
        return carry

    lax.fori_loop(0, jl, mix, 0)
    for c in range(cl):
        top, rest = split(m_ref[c].reshape(lanes, MODES))
        spread = (
            dot(bxr_ref[0], top, 1, 1) + dot(bxr_ref[1], top, 1, 1) + dot(bxr_ref[0], rest, 1, 1)
        )
        p_ref[:, c] = spread.astype(bf16).reshape(nx, xp, lanes)

    exchange(lambda d, h: p_ref.at[d], q_ref, send2, recv2)

    got = [q_ref[h * nx : (h + 1) * nx].reshape(MODES, xp, lanes) for h in range(ny)]
    got = jnp.concatenate(got, axis=2).astype(f32)
    got = jnp.swapaxes(got, 0, 1)[:xr].reshape(xr * MODES, ny * lanes).astype(bf16)
    got_ref[...] = got
    qs_ref[...] = dot(got, kyt_ref[0]) + dot(got, kyt_ref[1])

    def finish_field(x, carry):
        rows = pl.ds(pl.multiple_of(x * MODES, MODES), MODES)
        top, rest = split(qs_ref[rows, :])
        stack = jnp.concatenate([top, rest, top], axis=0)
        field = dot(stack, bzs_ref[...], 0, 0).reshape(channels, yr, zr)
        if back:
            values = [sig_ref[i, x] for i in range(channels)]
        else:
            values = [inc_ref[i, x].astype(f32) for i in range(channels)]
        for o in range(channels):
            total = field[o]
            for i in range(channels):
                total = total + (mix_ref[i, o] if back else mix_ref[o, i]) * values[i]
            if back:
                out_ref[o, x] = total.astype(bf16)
            else:
                total = total + bias_ref[0, o]
                cdf = 0.5 * (1.0 + lax.erf(total * 0.7071067811865476))
                out_ref[o, x] = cdf + total * jnp.exp(-0.5 * total * total) * 0.3989422804014327
        return carry

    lax.fori_loop(0, xr, finish_field, 0)


def ahead_kernel(
    act_ref, cot_ref, got_ref, got_back_ref, mix_ref, bias_ref, bzs_ref, kyt_ref, out_ref,
    pre_ref, back_ref,
):
    channels, xr, yr, zr = act_ref.shape
    pre_ref[...] = dot(got_ref[...], kyt_ref[0]) + dot(got_ref[...], kyt_ref[1])
    back_ref[...] = dot(got_back_ref[...], kyt_ref[0]) + dot(got_back_ref[...], kyt_ref[1])

    def field_of(ref, x):
        rows = pl.ds(pl.multiple_of(x * MODES, MODES), MODES)
        top, rest = split(ref[rows, :])
        stack = jnp.concatenate([top, rest, top], axis=0)
        return dot(stack, bzs_ref[...], 0, 0).reshape(channels, yr, zr)

    def step(x, carry):
        field = field_of(pre_ref, x)
        values = [act_ref[i, x].astype(f32) for i in range(channels)]
        signals = []
        for o in range(channels):
            total = field[o]
            for i in range(channels):
                total = total + mix_ref[o, i] * values[i]
            total = total + bias_ref[0, o]
            cdf = 0.5 * (1.0 + lax.erf(total * 0.7071067811865476))
            slope = cdf + total * jnp.exp(-0.5 * total * total) * 0.3989422804014327
            signals.append(cot_ref[o, x].astype(f32) * slope)
        field = field_of(back_ref, x)
        for o in range(channels):
            total = field[o]
            for i in range(channels):
                total = total + mix_ref[i, o] * signals[i]
            out_ref[o, x] = total.astype(bf16)
        return carry

    lax.fori_loop(0, xr, step, 0)


def ahead(activations, cotangent, got, got_back, mixing, bias, bzs, kyt):
    channels, xr, yr, zr = activations.shape
    vmem = pl.BlockSpec(memory_space=pltpu.VMEM)
    smem = pl.BlockSpec(memory_space=pltpu.SMEM)
    return pl.pallas_call(
        ahead_kernel,
        out_shape=jax.ShapeDtypeStruct(activations.shape, bf16),
        in_specs=[vmem] * 4 + [smem] * 2 + [vmem] * 2,
        out_specs=vmem,
        scratch_shapes=[pltpu.VMEM((xr * MODES, channels * yr), f32)] * 2,
        compiler_params=pltpu.CompilerParams(vmem_limit_bytes=50 * 2**20),
        cost_estimate=pl.CostEstimate(flops=10**9, bytes_accessed=10**7, transcendentals=10**6),
    )(activations, cotangent, got, got_back, mixing, bias, bzs, kyt)


def block_turn(back, nx, ny, collective, field, slope, weights, mixing, bias, tables):
    channels, xr, yr, zr = field.shape
    xp = -(-xr // 16) * 16
    cl, jl, n = MODES // nx, MODES // ny, nx * ny
    lanes = jl * channels
    vmem = pl.BlockSpec(memory_space=pltpu.VMEM)
    smem = pl.BlockSpec(memory_space=pltpu.SMEM)
    hbm = pl.BlockSpec(memory_space=pl.ANY)
    if back:
        args = (field, slope, weights, mixing, *tables)
        specs = [vmem, vmem, hbm, smem] + [vmem] * len(tables)
    else:
        args = (field, weights, mixing, bias, *tables)
        specs = [vmem, hbm, smem, smem] + [vmem] * len(tables)
    dma = pltpu.SemaphoreType.DMA
    return pl.pallas_call(
        functools.partial(kernel, back, nx, ny, xr),
        out_shape=(
            jax.ShapeDtypeStruct(field.shape, bf16 if back else f32),
            jax.ShapeDtypeStruct((cl, jl, channels, MODES), f32),
            jax.ShapeDtypeStruct((xr * MODES, ny * lanes), bf16),
        ),
        in_specs=specs,
        out_specs=(vmem, vmem, vmem),
        scratch_shapes=[
            pltpu.VMEM(weights.shape, f32),
            pltpu.VMEM(field.shape if back else (8, 128), f32),
            pltpu.VMEM((xr * MODES, channels * yr), bf16),
            pltpu.VMEM((xr * MODES, channels * yr), bf16),
            pltpu.VMEM((ny, nx, cl, xp, lanes), bf16),
            pltpu.VMEM((n, cl, xp, lanes), bf16),
            pltpu.VMEM((cl, jl, channels, MODES), f32),
            pltpu.VMEM((nx, cl, xp, lanes), bf16),
            pltpu.VMEM((n, cl, xp, lanes), bf16),
            pltpu.VMEM((xr * MODES, channels * yr), f32),
            dma((n,)), dma((n,)), dma((n,)), dma((n,)), dma,
        ],
        compiler_params=pltpu.CompilerParams(
            collective_id=collective, has_side_effects=True, vmem_limit_bytes=50 * 2**20
        ),
        cost_estimate=pl.CostEstimate(flops=10**9, bytes_accessed=2 * 10**7, transcendentals=10**6),
    )(*args)


def body(activations, cotangent, spectral_weights, pointwise, channel_bias):
    inputs = activations[0]
    channels, xr, yr, zr = inputs.shape
    nx, ny = lax.axis_size("gx"), lax.axis_size("gy")
    xp = -(-xr // 16) * 16
    bz = trig_basis(zr)
    bx = trig_basis(xr * nx).reshape(MODES, nx, xr)
    bx = np.concatenate([bx, np.zeros((MODES, nx, xp - xr))], axis=2).reshape(MODES, nx * xp)
    by = trig_basis(yr * ny).reshape(MODES, ny, yr)
    kron = np.einsum("jgy,ik->giyjk", by, np.eye(channels)).reshape(
        ny, channels * yr, MODES * channels
    )
    bzh = halves(bz)
    kh = halves(kron)
    gy = lax.axis_index("gy")
    ky = lax.dynamic_index_in_dim(jnp.asarray(np.swapaxes(kh, 0, 1)), gy, 0, False)
    kyt = lax.dynamic_index_in_dim(
        jnp.asarray(np.ascontiguousarray(np.transpose(kh, (1, 0, 3, 2)))), gy, 0, False
    )
    tables = (
        jnp.asarray(bzh),
        jnp.asarray(np.concatenate([bzh[0], bzh[0], bzh[1]], axis=0)),
        ky,
        kyt,
        jnp.asarray(halves(np.concatenate([bx] * ny, axis=1))),
        jnp.asarray(halves(bx.T)),
    )
    weights = spectral_weights[0]
    mixing = pointwise[0]
    following = [from_behind(v, "segment", -1) for v in (inputs, mixing, channel_bias)]
    slope, input_modes, got = block_turn(
        False, nx, ny, 0, inputs, None, weights, mixing, channel_bias, tables
    )
    next_got = from_behind(got, "segment", -1)
    segment_index = lax.axis_index("segment")
    segment_count = lax.axis_size("segment")
    incoming = cotangent
    kept_grad = jnp.zeros(cotangent.shape, bf16)
    kept_modes = jnp.zeros(input_modes.shape, f32)
    for turn_index in range(segment_count):
        active = segment_index == segment_count - 1 - turn_index
        input_grad, grad_modes, got_back = block_turn(
            True, nx, ny, 1 + turn_index, incoming, slope, weights, mixing, None, tables
        )
        kept_grad = jnp.where(active, input_grad, kept_grad)
        kept_modes = jnp.where(active, grad_modes, kept_modes)
        if turn_index == 0 and segment_count > 1:
            next_back = from_behind(got_back, "segment", -1)
            incoming = ahead(
                following[0], cotangent, next_got, next_back, following[1], following[2],
                tables[1], tables[3],
            )
        elif turn_index + 1 < segment_count:
            incoming = from_behind(input_grad, "segment", -1)
    input_modes = jnp.swapaxes(input_modes, 0, 1)
    kept_modes = jnp.swapaxes(kept_modes, 0, 1)
    weight_grad = input_modes[:, :, :, None, :] * kept_modes[:, :, None, :, :]
    return (kept_grad[None], weight_grad[None])


def solution(mesh):
    return jax.shard_map(
        body,
        mesh=mesh,
        in_specs=(
            P("segment", "groups", "gx", "gy", None),
            P("groups", "gx", "gy", None),
            P("segment", "gy", "gx", None, None, None),
            P("segment", None, None),
            P("segment", None),
        ),
        out_specs=(
            P("segment", "groups", "gx", "gy", None),
            P("segment", "gy", "gx", "groups", None, None),
        ),
        check_vma=False,
    )
```

```python
import functools
import math

import jax
import jax.numpy as jnp
import ml_dtypes
import numpy as np
from jax import lax
from jax.experimental import pallas as pl
from jax.experimental.pallas import tpu as pltpu
from jax.sharding import PartitionSpec as P

MODES = 32
f32, bf16 = jnp.float32, jnp.bfloat16


def from_behind(block, axis, distance):
    devices = range(lax.axis_size(axis))
    route = [(i - distance, i) for i in devices if i - distance in devices]
    return lax.ppermute(block, axis, route)


def trig_basis(length):
    half = MODES // 2
    freqs = np.arange(half)[:, None]
    points = np.arange(length)[None, :]
    step = 2.0 * math.pi / length
    rows = np.concatenate(
        [np.cos((freqs * points % length) * step), np.sin(((freqs + 1) * points % length) * step)]
    )
    scales = np.where(np.arange(MODES) == 0, 1.0 / math.sqrt(length), math.sqrt(2.0 / length))
    return rows * scales[:, None]


def halves(matrix):
    matrix = np.asarray(matrix, np.float32)
    top = matrix.astype(ml_dtypes.bfloat16)
    rest = (matrix - top.astype(np.float32)).astype(ml_dtypes.bfloat16)
    return np.stack([top, rest])


def split(value):
    top = value.astype(bf16)
    return top, (value - top.astype(f32)).astype(bf16)


def dot(a, b, ca=1, cb=0):
    return lax.dot_general(a, b, (((ca,), (cb,)), ((), ())), preferred_element_type=f32)


def kernel(
    back, nx, ny, xr, *refs
):
    if back:
        (inc_ref, slope_ref, w_hbm, mix_ref, bz_ref, bzs_ref, ky_ref, kyt_ref, bx_ref, bxr_ref,
         out_ref, modes_ref, got_ref, *scratch) = refs
    else:
        (inc_ref, w_hbm, mix_ref, bias_ref, bz_ref, bzs_ref, ky_ref, kyt_ref, bx_ref, bxr_ref,
         out_ref, modes_ref, got_ref, *scratch) = refs
    (w_ref, sig_ref, ghi_ref, glo_ref, s_ref, r_ref, m_ref, p_ref, q_ref, qs_ref,
     send1, recv1, send2, recv2, wsem) = scratch
    channels, _, yr, zr = inc_ref.shape
    cl, jl, xp = MODES // nx, MODES // ny, r_ref.shape[2]
    n = nx * ny
    lanes = jl * channels
    gx, gy = lax.axis_index("gx"), lax.axis_index("gy")
    me = gx * ny + gy

    wcopy = pltpu.make_async_copy(w_hbm, w_ref, wsem)
    wcopy.start()

    barrier = pltpu.get_barrier_semaphore()

    def greet(k, carry):
        peer = lax.rem(me + k, n)
        pl.semaphore_signal(
            barrier, inc=1,
            device_id={"gx": peer // ny, "gy": lax.rem(peer, ny)},
            device_id_type=pl.DeviceIdType.MESH,
        )
        return carry

    lax.fori_loop(1, n, greet, 0)

    def along_z(x, carry):
        if back:
            signal = inc_ref[:, x].astype(f32) * slope_ref[:, x]
            sig_ref[:, x] = signal
            block = signal.astype(bf16)
        else:
            block = inc_ref[:, x]
        block = block.reshape(channels * yr, zr)
        g = dot(bz_ref[0], block, 1, 1) + dot(bz_ref[1], block, 1, 1)
        ghi, glo = split(g)
        rows = pl.ds(pl.multiple_of(x * MODES, MODES), MODES)
        ghi_ref[rows, :] = ghi
        glo_ref[rows, :] = glo
        return carry

    lax.fori_loop(0, xr, along_z, 0)
    ghi = ghi_ref[...]
    t = dot(ghi, ky_ref[0]) + dot(ghi, ky_ref[1]) + dot(glo_ref[...], ky_ref[0])
    t = jnp.swapaxes(t.reshape(xr, MODES, ny * lanes), 0, 1)
    if xp > xr:
        t = jnp.concatenate([t, jnp.zeros((MODES, xp - xr, ny * lanes), f32)], axis=1)
    t = t.astype(bf16)
    for h in range(ny):
        s_ref[h] = t[:, :, h * lanes : (h + 1) * lanes].reshape(nx, cl, xp, lanes)

    pl.semaphore_wait(barrier, n - 1)

    def exchange(source, target, send, recv):
        def copy_to(peer, slot_of):
            return pltpu.make_async_remote_copy(
                src_ref=source(peer // ny, lax.rem(peer, ny)),
                dst_ref=target.at[lax.rem(slot_of, ny) * nx + slot_of // ny],
                send_sem=send.at[peer],
                recv_sem=recv.at[slot_of],
                device_id={"gx": peer // ny, "gy": lax.rem(peer, ny)},
                device_id_type=pl.DeviceIdType.MESH,
            )

        def begin(k, carry):
            copy_to(lax.rem(me + k, n), me).start()
            return carry

        def finish(k, carry):
            copy_to(lax.rem(me + k, n), me).wait_send()
            peer = lax.rem(me + n - k, n)
            copy_to(peer, peer).wait_recv()
            return carry

        lax.fori_loop(1, n, begin, 0)
        target[gy * nx + gx] = source(gx, gy)[...]
        lax.fori_loop(1, n, finish, 0)

    exchange(lambda d, h: s_ref.at[h, d], r_ref, send1, recv1)

    for c in range(cl):
        part = r_ref[:, c].reshape(n * xp, lanes)
        own = dot(bx_ref[0], part) + dot(bx_ref[1], part)
        modes_ref[c] = own.T.reshape(jl, channels, MODES)
    wcopy.wait()

    def mix(j, carry):
        for c in range(cl):
            own = modes_ref[c, j]
            weight = w_ref[j, c]
            if back:
                m_ref[c, j] = jnp.sum(weight * own[None], axis=1)
            else:
                m_ref[c, j] = jnp.sum(weight * own[:, None, :], axis=0)
        return carry

    lax.fori_loop(0, jl, mix, 0)
    for c in range(cl):
        top, rest = split(m_ref[c].reshape(lanes, MODES))
        spread = (
            dot(bxr_ref[0], top, 1, 1) + dot(bxr_ref[1], top, 1, 1) + dot(bxr_ref[0], rest, 1, 1)
        )
        p_ref[:, c] = spread.astype(bf16).reshape(nx, xp, lanes)

    exchange(lambda d, h: p_ref.at[d], q_ref, send2, recv2)

    got = [q_ref[h * nx : (h + 1) * nx].reshape(MODES, xp, lanes) for h in range(ny)]
    got = jnp.concatenate(got, axis=2).astype(f32)
    got = jnp.swapaxes(got, 0, 1)[:xr].reshape(xr * MODES, ny * lanes).astype(bf16)
    got_ref[...] = got
    qs_ref[...] = dot(got, kyt_ref[0]) + dot(got, kyt_ref[1])

    def finish_field(x, carry):
        rows = pl.ds(pl.multiple_of(x * MODES, MODES), MODES)
        top, rest = split(qs_ref[rows, :])
        stack = jnp.concatenate([top, rest, top], axis=0)
        field = dot(stack, bzs_ref[...], 0, 0).reshape(channels, yr, zr)
        if back:
            values = [sig_ref[i, x] for i in range(channels)]
        else:
            values = [inc_ref[i, x].astype(f32) for i in range(channels)]
        for o in range(channels):
            total = field[o]
            for i in range(channels):
                total = total + (mix_ref[i, o] if back else mix_ref[o, i]) * values[i]
            if back:
                out_ref[o, x] = total.astype(bf16)
            else:
                total = total + bias_ref[0, o]
                cdf = 0.5 * (1.0 + lax.erf(total * 0.7071067811865476))
                out_ref[o, x] = cdf + total * jnp.exp(-0.5 * total * total) * 0.3989422804014327
        return carry

    lax.fori_loop(0, xr, finish_field, 0)


def ahead_kernel(
    act_ref, cot_ref, got_ref, got_back_ref, mix_ref, bias_ref, bzs_ref, kyt_ref, out_ref,
    pre_ref, back_ref,
):
    channels, xr, yr, zr = act_ref.shape
    pre_ref[...] = dot(got_ref[...], kyt_ref[0]) + dot(got_ref[...], kyt_ref[1])
    back_ref[...] = dot(got_back_ref[...], kyt_ref[0]) + dot(got_back_ref[...], kyt_ref[1])

    def field_of(ref, x):
        rows = pl.ds(pl.multiple_of(x * MODES, MODES), MODES)
        top, rest = split(ref[rows, :])
        stack = jnp.concatenate([top, rest, top], axis=0)
        return dot(stack, bzs_ref[...], 0, 0).reshape(channels, yr, zr)

    def step(x, carry):
        field = field_of(pre_ref, x)
        values = [act_ref[i, x].astype(f32) for i in range(channels)]
        signals = []
        for o in range(channels):
            total = field[o]
            for i in range(channels):
                total = total + mix_ref[o, i] * values[i]
            total = total + bias_ref[0, o]
            cdf = 0.5 * (1.0 + lax.erf(total * 0.7071067811865476))
            slope = cdf + total * jnp.exp(-0.5 * total * total) * 0.3989422804014327
            signals.append(cot_ref[o, x].astype(f32) * slope)
        field = field_of(back_ref, x)
        for o in range(channels):
            total = field[o]
            for i in range(channels):
                total = total + mix_ref[i, o] * signals[i]
            out_ref[o, x] = total.astype(bf16)
        return carry

    lax.fori_loop(0, xr, step, 0)


def ahead(activations, cotangent, got, got_back, mixing, bias, bzs, kyt):
    channels, xr, yr, zr = activations.shape
    vmem = pl.BlockSpec(memory_space=pltpu.VMEM)
    smem = pl.BlockSpec(memory_space=pltpu.SMEM)
    return pl.pallas_call(
        ahead_kernel,
        out_shape=jax.ShapeDtypeStruct(activations.shape, bf16),
        in_specs=[vmem] * 4 + [smem] * 2 + [vmem] * 2,
        out_specs=vmem,
        scratch_shapes=[pltpu.VMEM((xr * MODES, channels * yr), f32)] * 2,
        compiler_params=pltpu.CompilerParams(vmem_limit_bytes=50 * 2**20),
        cost_estimate=pl.CostEstimate(flops=10**9, bytes_accessed=10**7, transcendentals=10**6),
    )(activations, cotangent, got, got_back, mixing, bias, bzs, kyt)


def block_turn(back, nx, ny, collective, field, slope, weights, mixing, bias, tables):
    channels, xr, yr, zr = field.shape
    xp = -(-xr // 16) * 16
    cl, jl, n = MODES // nx, MODES // ny, nx * ny
    lanes = jl * channels
    vmem = pl.BlockSpec(memory_space=pltpu.VMEM)
    smem = pl.BlockSpec(memory_space=pltpu.SMEM)
    hbm = pl.BlockSpec(memory_space=pl.ANY)
    if back:
        args = (field, slope, weights, mixing, *tables)
        specs = [vmem, vmem, hbm, smem] + [vmem] * len(tables)
    else:
        args = (field, weights, mixing, bias, *tables)
        specs = [vmem, hbm, smem, smem] + [vmem] * len(tables)
    dma = pltpu.SemaphoreType.DMA
    return pl.pallas_call(
        functools.partial(kernel, back, nx, ny, xr),
        out_shape=(
            jax.ShapeDtypeStruct(field.shape, bf16 if back else f32),
            jax.ShapeDtypeStruct((cl, jl, channels, MODES), f32),
            jax.ShapeDtypeStruct((xr * MODES, ny * lanes), bf16),
        ),
        in_specs=specs,
        out_specs=(vmem, vmem, vmem),
        scratch_shapes=[
            pltpu.VMEM(weights.shape, f32),
            pltpu.VMEM(field.shape if back else (8, 128), f32),
            pltpu.VMEM((xr * MODES, channels * yr), bf16),
            pltpu.VMEM((xr * MODES, channels * yr), bf16),
            pltpu.VMEM((ny, nx, cl, xp, lanes), bf16),
            pltpu.VMEM((n, cl, xp, lanes), bf16),
            pltpu.VMEM((cl, jl, channels, MODES), f32),
            pltpu.VMEM((nx, cl, xp, lanes), bf16),
            pltpu.VMEM((n, cl, xp, lanes), bf16),
            pltpu.VMEM((xr * MODES, channels * yr), f32),
            dma((n,)), dma((n,)), dma((n,)), dma((n,)), dma,
        ],
        compiler_params=pltpu.CompilerParams(
            collective_id=collective, has_side_effects=True, vmem_limit_bytes=50 * 2**20
        ),
        cost_estimate=pl.CostEstimate(flops=10**9, bytes_accessed=2 * 10**7, transcendentals=10**6),
    )(*args)


def body(activations, cotangent, spectral_weights, pointwise, channel_bias):
    inputs = activations[0]
    channels, xr, yr, zr = inputs.shape
    nx, ny = lax.axis_size("gx"), lax.axis_size("gy")
    xp = -(-xr // 16) * 16
    bz = trig_basis(zr)
    bx = trig_basis(xr * nx).reshape(MODES, nx, xr)
    bx = np.concatenate([bx, np.zeros((MODES, nx, xp - xr))], axis=2).reshape(MODES, nx * xp)
    by = trig_basis(yr * ny).reshape(MODES, ny, yr)
    kron = np.einsum("jgy,ik->giyjk", by, np.eye(channels)).reshape(
        ny, channels * yr, MODES * channels
    )
    bzh = halves(bz)
    kh = halves(kron)
    gy = lax.axis_index("gy")
    ky = lax.dynamic_index_in_dim(jnp.asarray(np.swapaxes(kh, 0, 1)), gy, 0, False)
    kyt = lax.dynamic_index_in_dim(
        jnp.asarray(np.ascontiguousarray(np.transpose(kh, (1, 0, 3, 2)))), gy, 0, False
    )
    tables = (
        jnp.asarray(bzh),
        jnp.asarray(np.concatenate([bzh[0], bzh[0], bzh[1]], axis=0)),
        ky,
        kyt,
        jnp.asarray(halves(np.concatenate([bx] * ny, axis=1))),
        jnp.asarray(halves(bx.T)),
    )
    weights = spectral_weights[0]
    mixing = pointwise[0]
    following = [from_behind(v, "segment", -1) for v in (inputs, mixing, channel_bias)]
    slope, input_modes, got = block_turn(
        False, nx, ny, 0, inputs, None, weights, mixing, channel_bias, tables
    )
    next_got = from_behind(got, "segment", -1)
    segment_index = lax.axis_index("segment")
    segment_count = lax.axis_size("segment")
    incoming, following[1], following[2] = lax.optimization_barrier(
        (cotangent, following[1], following[2])
    )
    kept_grad = jnp.zeros(cotangent.shape, bf16)
    kept_modes = jnp.zeros(input_modes.shape, f32)
    for turn_index in range(segment_count):
        active = segment_index == segment_count - 1 - turn_index
        input_grad, grad_modes, got_back = block_turn(
            True, nx, ny, 1 + turn_index, incoming, slope, weights, mixing, None, tables
        )
        kept_grad = jnp.where(active, input_grad, kept_grad)
        kept_modes = jnp.where(active, grad_modes, kept_modes)
        if turn_index == 0 and segment_count > 1:
            next_back = from_behind(got_back, "segment", -1)
            incoming = ahead(
                following[0], cotangent, next_got, next_back, following[1], following[2],
                tables[1], tables[3],
            )
        elif turn_index + 1 < segment_count:
            incoming = from_behind(input_grad, "segment", -1)
    input_modes = jnp.swapaxes(input_modes, 0, 1)
    kept_modes = jnp.swapaxes(kept_modes, 0, 1)
    weight_grad = input_modes[:, :, :, None, :] * kept_modes[:, :, None, :, :]
    return (kept_grad[None], weight_grad[None])


def solution(mesh):
    return jax.shard_map(
        body,
        mesh=mesh,
        in_specs=(
            P("segment", "groups", "gx", "gy", None),
            P("groups", "gx", "gy", None),
            P("segment", "gy", "gx", None, None, None),
            P("segment", None, None),
            P("segment", None),
        ),
        out_specs=(
            P("segment", "groups", "gx", "gy", None),
            P("segment", "gy", "gx", "groups", None, None),
        ),
        check_vma=False,
    )
```
